256 devices in a mesh: tile: 16 (over z_hi, y), pulse: 16 (over x, z_lo, core).
Axes of the slice: x: 4, y: 4, z: 8 (z_hi: 4, z_lo: 2; z = z_hi * 2 + z_lo), core: 2. Of those that a mesh axis runs over, the one named last changes fastest.
Arguments:
- profile: float32 [2, 128, 16384], P(None, 'pulse', 'tile'), may hold values from -6 to 6
- base_bin: int32 [128, 65536], P('pulse', 'tile'), may hold values from 0 to 16376, as said below
- tap_offset: int32 [128, 65536], P('pulse', 'tile'), may hold values from 0 to 15
Outputs:
- image: float32 [2, 65536], P(None, ('tile', 'pulse'))
The draws below stay inside these ranges and needn't reach their ends.
Inputs may be any that keep to these rules, and one draw needn't show every extreme that they name: `base_bin`: for each pulse and each aligned block of 256 pixels, the base bins lie within 505 consecutive bins, and in every block they span exactly that many.
All inputs are finite; a program needn't handle non-finite values.
Results may differ from the reference program's by a relative error of at most 0.0003.
Values sent between devices are 32-bit elements; how exact they have to be, the bound alone decides.
No kernel may reach another device: no remote copies, remote signals or barrier semaphores. Data moves between devices by JAX's collectives and lax.ppermute only.
A program may use at most 256 MiB of HBM per device.

```python
import math
import jax
import jax.numpy as jnp
from jax import lax

BINS = 16384
TAPS = 8
FRAC = 16
WINDOW = 512
BLOCK = 256
PULSES = 128
PIXELS = 65536


def draw_base_bin(key, part):
    block_count = PIXELS // BLOCK
    span = WINDOW - TAPS + 1
    first_key, inner_key, low_key, high_key = jax.random.split(jax.random.fold_in(key, 17), 4)
    starts = jax.random.randint(first_key, (PULSES, block_count, 1), 0, BINS - WINDOW + 1)
    starts = starts.at[0, 0, 0].set(0)
    starts = starts.at[PULSES - 1, block_count - 1, 0].set(BINS - WINDOW)
    inner = jax.random.randint(inner_key, (PULSES, block_count, BLOCK), 0, span)
    low_spot = jax.random.randint(low_key, (PULSES, block_count, 1), 0, BLOCK)
    step_ahead = jax.random.randint(high_key, (PULSES, block_count, 1), 1, BLOCK)
    high_spot = (low_spot + step_ahead) % BLOCK
    places = jnp.arange(BLOCK, dtype=jnp.int32)[None, None, :]
    inner = jnp.where(places == low_spot, 0, jnp.where(places == high_spot, span - 1, inner))
    return (starts + inner).reshape(PULSES, PIXELS).astype(jnp.int32)


def with_ends(array, key, low, top_value):
    dims = array.shape
    index_at = [jax.random.randint(jax.random.fold_in(key, axis), (), 0, dims[axis]) for axis in range(len(dims))]
    array = array.at[tuple(index_at)].set(low)
    longest = dims.index(max(dims))
    index_at[longest] = (index_at[longest] + 1) % dims[longest]
    return array.at[tuple(index_at)].set(top_value)


def shard_levels(rng, extent, shards, low, largest):
    def one(dim, shards_of):
        steps = jax.random.uniform(jax.random.fold_in(jax.random.fold_in(rng, 6), dim), (shards_of,), jnp.float32, low / len(shards), largest / len(shards))
        return jnp.repeat(jnp.exp(steps), extent[dim] // shards_of).reshape((-1,) + (1,) * (len(extent) - dim - 1))

    level = one(*shards[0])
    for cut in shards[1:]:
        level = level * one(*cut)
    return level


def gaussian(own_key, shape, width, most, shards=(), kind=jnp.bfloat16):
    loudness = shard_levels(own_key, shape, shards, -0.22, 0.18) if shards else 1.0
    entries = jax.random.normal(own_key, shape, jnp.float32) * width * loudness
    return jnp.minimum(jnp.maximum(entries, -most), most).astype(kind)


def setup_inputs(seed: int = 0) -> dict:
    keys = jax.random.split(jax.random.key(seed), 4)
    return {
        "profile": gaussian(keys[0], (2, PULSES, BINS), 1.0, 6.0, ((1, 16), (2, 16)), jnp.float32),
        "base_bin": draw_base_bin(jax.random.fold_in(keys[3], 71), 0),
        "tap_offset": with_ends(jax.random.randint(keys[2], (PULSES, PIXELS), 0, FRAC), jax.random.fold_in(keys[2], 1), 0, FRAC - 1).astype(jnp.int32),
    }


def tap_table():
    frac_part = jnp.arange(FRAC, dtype=jnp.float32)[:, None] / FRAC
    shift = jnp.arange(TAPS, dtype=jnp.float32)[None, :] - (TAPS // 2 - 1)
    offset = shift - frac_part
    values = jnp.sinc(offset) * (0.5 + 0.5 * jnp.cos(math.pi * offset / (TAPS // 2)))
    return values / lax.optimization_barrier(jnp.sum(values, axis=1, keepdims=True))

def phase_angle(bins, offsets):
    fine = bins * FRAC + offsets
    steps = fine * 2861 % 4096
    return steps.astype(jnp.float32) * (2.0 * math.pi / 4096.0)

def reference(profile, base_bin, tap_offset):
    table = tap_table()

    def one_pulse(total, items):
        trace, bins, offsets = items
        accum = jnp.zeros((2, bins.shape[0]), jnp.float32)
        for shift in range(TAPS):
            values = jnp.take(trace, (bins + shift).astype(jnp.int32), axis=1)
            weight = jnp.take(table[:, shift], offsets.astype(jnp.int32), axis=0)
            accum = accum + weight[None, :] * values
        angle = phase_angle(bins, offsets)
        cosine = jnp.cos(angle)
        sine = jnp.sin(angle)
        real_part = accum[0] * cosine - accum[1] * sine
        imag_part = accum[0] * sine + accum[1] * cosine
        return (total + jnp.stack([real_part, imag_part]), None)
    start = jnp.zeros((2, base_bin.shape[1]), jnp.float32)
    traces = jnp.transpose(profile, (1, 0, 2))
    total, _ = lax.scan(one_pulse, start, (traces, base_bin, tap_offset))
    return total * (1.0 / math.sqrt(PULSES))
```

```python
import math

import jax
import jax.numpy as jnp
from jax import lax
from jax.experimental import pallas as pl
from jax.experimental.pallas import tpu as pltpu
from jax.sharding import PartitionSpec as P

TAPS = 8
FRAC = 16
BLOCK = 256
LANES = 128
REACH = 5
SIDE = 4


def tap_table():
    frac_part = jnp.arange(FRAC, dtype=jnp.float32)[:, None] / FRAC
    shift = jnp.arange(TAPS, dtype=jnp.float32)[None, :] - (TAPS // 2 - 1)
    offset = shift - frac_part
    values = jnp.sinc(offset) * (0.5 + 0.5 * jnp.cos(math.pi * offset / (TAPS // 2)))
    values = values / jnp.sum(values, axis=1, keepdims=True)
    return jnp.pad(values.T, ((0, 0), (0, LANES - FRAC)))


def lane_take(row, index):
    return jnp.take_along_axis(row, index, axis=1, mode="promise_in_bounds")


def cos_sin(steps):
    quarter = (steps + 512) >> 10
    x = (steps - (quarter << 10)).astype(jnp.float32) * (2.0 * math.pi / 4096.0)
    y = x * x
    s = x * (1.0 + y * (-1.0 / 6.0 + y * (1.0 / 120.0 + y * (-1.0 / 5040.0 + y * (1.0 / 362880.0)))))
    c = 1.0 + y * (-0.5 + y * (1.0 / 24.0 + y * (-1.0 / 720.0 + y * (1.0 / 40320.0))))
    odd = (quarter & 1) == 1
    cosine = jnp.where(odd, s, c)
    sine = jnp.where(odd, c, s)
    cosine = jnp.where(((quarter + 1) & 2) == 2, -cosine, cosine)
    sine = jnp.where((quarter & 2) == 2, -sine, sine)
    return cosine, sine


def prepare_kernel(table_ref, first_ref, bins_ref, offsets_ref, rel_ref, weight_ref, cos_ref, sin_ref):
    pixels = bins_ref.shape[1]
    tables = [jnp.broadcast_to(table_ref[j : j + 1, :], (8, LANES)) for j in range(TAPS)]
    for part in range(pixels // LANES):
        lanes = pl.ds(part * LANES, LANES)
        block = part * LANES // BLOCK
        bins = bins_ref[:, lanes]
        offsets = offsets_ref[:, lanes]
        rel_ref[:, lanes] = bins - first_ref[:, block : block + 1] * LANES
        steps = ((bins * FRAC + offsets) * 2861) & 4095
        cosine, sine = cos_sin(steps)
        cos_ref[:, lanes] = cosine
        sin_ref[:, lanes] = sine
        for j in range(TAPS):
            weight_ref[j, :, lanes] = lane_take(tables[j], offsets)


def project_kernel(scale, place_ref, first_ref, p0, p1, p2, p3, rel_ref, weight_ref, cos_ref, sin_ref, out_ref, whole, window):
    pulses, pixels = rel_ref.shape
    bins = p0.shape[3]
    my_z, my_y = place_ref[0], place_ref[1]
    for dy, piece in enumerate((p0, p1, p2, p3)):
        for dz in range(SIDE):
            owner = ((my_z - dz) & (SIDE - 1)) * SIDE + ((my_y - dy) & (SIDE - 1))
            for c in range(2):
                for t in range(bins // LANES):
                    whole[c, owner * (bins // LANES) + t] = piece[dz, c, :, t * LANES : (t + 1) * LANES]
    for block in range(pixels // BLOCK):
        for s in range(pulses):
            first = first_ref[s, block]
            for c in range(2):
                for r in range(REACH):
                    window[block, c, r, s : s + 1, :] = whole[c, first + r, s : s + 1, :]
    for block in range(pixels // BLOCK):
        for half in range(BLOCK // LANES):
            lanes = pl.ds(block * BLOCK + half * LANES, LANES)
            rel = rel_ref[:, lanes]
            real = jnp.zeros((pulses, LANES), jnp.float32)
            imag = jnp.zeros((pulses, LANES), jnp.float32)
            for j in range(TAPS):
                index = rel + j
                lane = index & (LANES - 1)
                row = index >> 7
                got = [lane_take(window[block, c, 0], lane) for c in range(2)]
                for r in range(1, REACH):
                    here = row == r
                    for c in range(2):
                        got[c] = jnp.where(here, lane_take(window[block, c, r], lane), got[c])
                weight = weight_ref[j, :, lanes]
                real = real + weight * got[0]
                imag = imag + weight * got[1]
            cosine = cos_ref[:, lanes]
            sine = sin_ref[:, lanes]
            out_ref[block, half : half + 1, :] = jnp.sum(real * cosine - imag * sine, axis=0, keepdims=True) * scale
            out_ref[block, 2 + half : 3 + half, :] = jnp.sum(real * sine + imag * cosine, axis=0, keepdims=True) * scale


def shifted(dz, dy):
    return [
        (z * SIDE + y, (z + dz) % SIDE * SIDE + (y + dy) % SIDE) for z in range(SIDE) for y in range(SIDE)
    ]


def local(profile, base_bin, tap_offset):
    pulses, pixels = base_bin.shape
    blocks = pixels // BLOCK
    bins = profile.shape[2]
    scale = 1.0 / math.sqrt(pulses * lax.axis_size("pulse"))
    me = lax.axis_index("tile")
    place = jnp.stack([me // SIDE, me % SIDE]).astype(jnp.int32)

    column = [profile] + [lax.ppermute(profile, "tile", shifted(dz, 0)) for dz in range(1, SIDE)]
    column = jnp.stack(column)
    pieces = [column] + [lax.ppermute(column, "tile", shifted(0, dy)) for dy in range(1, SIDE)]

    first = jnp.min(base_bin.reshape(pulses, blocks, BLOCK), axis=2) >> 7
    vmem = pl.BlockSpec(memory_space=pltpu.VMEM)
    smem = pl.BlockSpec(memory_space=pltpu.SMEM)
    rel, weight, cosine, sine = pl.pallas_call(
        prepare_kernel,
        out_shape=[
            jax.ShapeDtypeStruct((pulses, pixels), jnp.int32),
            jax.ShapeDtypeStruct((TAPS, pulses, pixels), jnp.float32),
            jax.ShapeDtypeStruct((pulses, pixels), jnp.float32),
            jax.ShapeDtypeStruct((pulses, pixels), jnp.float32),
        ],
        in_specs=[vmem] * 4,
        out_specs=[vmem] * 4,
        cost_estimate=pl.CostEstimate(flops=pulses * pixels * 300, bytes_accessed=pulses * pixels * 52, transcendentals=0),
        compiler_params=pltpu.CompilerParams(vmem_limit_bytes=16 << 20),
        name="prepare",
    )(tap_table(), first, base_bin, tap_offset)
    partial_image = pl.pallas_call(
        lambda *refs: project_kernel(scale, *refs),
        out_shape=jax.ShapeDtypeStruct((blocks, 4, LANES), jnp.float32),
        in_specs=[smem] * 2 + [vmem] * 8,
        out_specs=vmem,
        scratch_shapes=[
            pltpu.VMEM((2, SIDE * SIDE * bins // LANES + REACH, pulses, LANES), jnp.float32),
            pltpu.VMEM((blocks, 2, REACH, pulses, LANES), jnp.float32),
        ],
        compiler_params=pltpu.CompilerParams(vmem_limit_bytes=32 << 20),
        name="project",
    )(place, first, *pieces, rel, weight, cosine, sine)
    parts = lax.all_to_all(partial_image, "pulse", 0, 0, tiled=True)
    return jnp.sum(parts, axis=0).reshape(2, BLOCK)


def solution(mesh):
    return jax.shard_map(
        local,
        mesh=mesh,
        in_specs=(P(None, "pulse", "tile"), P("pulse", "tile"), P("pulse", "tile")),
        out_specs=P(None, ("tile", "pulse")),
        check_vma=False,
    )
```

```python
import math

import jax
import jax.numpy as jnp
from jax import lax
from jax.experimental import pallas as pl
from jax.experimental.pallas import tpu as pltpu
from jax.sharding import Mesh
from jax.sharding import PartitionSpec as P

TAPS = 8
FRAC = 16
BLOCK = 256
LANES = 128
SUBLANES = 8
SIDE = 4
AXES = ("far", "near", "x", "pair", "core")
SIZES = (4, 4, 4, 2, 2)


def tap_table():
    frac_part = jnp.arange(FRAC, dtype=jnp.float32)[:, None] / FRAC
    shift = jnp.arange(TAPS, dtype=jnp.float32)[None, :] - (TAPS // 2 - 1)
    offset = shift - frac_part
    values = jnp.sinc(offset) * (0.5 + 0.5 * jnp.cos(math.pi * offset / (TAPS // 2)))
    values = values / jnp.sum(values, axis=1, keepdims=True)
    return values.reshape(1, FRAC * TAPS)


def lane_take(row, index):
    return jnp.take_along_axis(row, index, axis=1, mode="promise_in_bounds")


def spread(row):
    return jnp.broadcast_to(row, (SUBLANES, LANES))


def cos_sin(steps):
    quarter = (steps + 512) >> 10
    x = (steps - (quarter << 10)).astype(jnp.float32) * (2.0 * math.pi / 4096.0)
    y = x * x
    s = x * (1.0 + y * (-1.0 / 6.0 + y * (1.0 / 120.0 + y * (-1.0 / 5040.0 + y * (1.0 / 362880.0)))))
    c = 1.0 + y * (-0.5 + y * (1.0 / 24.0 + y * (-1.0 / 720.0 + y * (1.0 / 40320.0))))
    odd = (quarter & 1) == 1
    cosine = jnp.where(odd, s, c)
    sine = jnp.where(odd, c, s)
    cosine = jnp.where(((quarter + 1) & 2) == 2, -cosine, cosine)
    sine = jnp.where((quarter & 2) == 2, -sine, sine)
    return cosine, sine


def arrange_kernel(near_ref, shard_ref, bins_ref, offsets_ref, *refs):
    *index_refs, out_ref, tiles = refs
    near = near_ref[0]
    lane = lax.broadcasted_iota(jnp.int32, (SUBLANES, LANES), 1)
    source = (lane & 15) * TAPS
    part = lane >> 4
    each = out_ref.shape[2]
    for c in range(2):
        rows = [shard_ref[c, :, t * LANES : (t + 1) * LANES] for t in range(TAPS)]
        for v in range(TAPS):
            got = lane_take(rows[0], source + v)
            for t in range(1, TAPS):
                got = jnp.where(part == t, lane_take(rows[t], source + v), got)
            tiles[c, :, v, :] = got
    quarters = SUBLANES // each
    length = index_refs[0].shape[2]
    for step, index_ref in enumerate(index_refs):
        for k, ref in enumerate((bins_ref, offsets_ref)):
            for p in range(each):
                pulse = pl.ds((near ^ step) * each + p, 1)
                for q in range(quarters):
                    row = p * quarters + q
                    index_ref[k, row : row + 1, :] = ref[pulse, q * length : (q + 1) * length]
    for c in range(2):
        for place in range(SIDE):
            for p in range(each):
                tile = tiles[c, place * each + p]
                for far in range(SIDE):
                    out_ref[far * SIDE + place, c, p] = tile


def prepare_kernel(scale, table_ref, index_ref, first_ref, real_ref, imag_ref, lane_ref):
    tiles, _, rows, length = index_ref.shape
    halves = BLOCK // LANES
    table = spread(table_ref[:, :])
    phase = lax.broadcasted_iota(jnp.int32, (SUBLANES, LANES), 0)
    for tile in range(tiles):
        for part in range(length // LANES):
            lanes = pl.ds(part * LANES, LANES)
            bins = index_ref[tile, 0, :, lanes]
            least = bins if part % halves == 0 else jnp.minimum(least, bins)
            if part % halves == halves - 1:
                block = part // halves
                lowest = jnp.min(least.astype(jnp.float32), axis=1, keepdims=True)
                first_ref[tile, :, block : block + 1] = lowest.astype(jnp.int32)
            fine = bins * FRAC + index_ref[tile, 1, :, lanes]
            cosine, sine = cos_sin((fine * 2861) & 4095)
            cosine, sine = cosine * scale, sine * scale
            for s in range(rows):
                fine_s = spread(fine[s : s + 1])
                bins_s = fine_s >> 4
                weight = lane_take(table, ((fine_s & 15) << 3) + ((phase - bins_s) & 7))
                real_ref[tile, s, part] = weight * spread(cosine[s : s + 1])
                imag_ref[tile, s, part] = weight * spread(sine[s : s + 1])
                lane_ref[tile, s, part] = ((bins_s - phase + 7) >> 3) & (LANES - 1)


def row_sums(values):
    row = lax.broadcasted_iota(jnp.int32, (SUBLANES, LANES), 0)
    low = (row & 4) == 0
    values = [jnp.where(low, a, b) + pltpu.roll(jnp.where(low, b, a), 4, 0) for a, b in zip(values[:4], values[4:])]
    for step in (2, 1):
        low = (row & step) == 0
        values = [
            jnp.where(low, a + pltpu.roll(a, SUBLANES - step, 0), b + pltpu.roll(b, step, 0))
            for a, b in zip(values[:step], values[step:])
        ]
    return values[0]


def project_kernel(near_ref, first_ref, whole, real_ref, imag_ref, lane_ref, out_ref):
    tiles, rows, parts = real_ref.shape[:3]
    owners, _, each = whole.shape[:3]
    quarters = rows // each
    halves = BLOCK // LANES
    column = lax.broadcasted_iota(jnp.int32, (SUBLANES, LANES), 1)
    for tile in range(tiles):
        for quarter in range(quarters):
            sums = []
            for block in range(parts // halves):
                total = [[jnp.zeros((SUBLANES, LANES), jnp.float32) for _ in range(halves)] for _ in range(2)]
                for p in range(each):
                    row = p * quarters + quarter
                    first = first_ref[tile, row, block]
                    owner = first >> 10
                    after = jnp.minimum(owner + 1, owners - 1)
                    here = column >= ((first >> 3) & (LANES - 1))
                    table = [jnp.where(here, whole[owner, c, p], whole[after, c, p]) for c in range(2)]
                    for half in range(halves):
                        part = block * halves + half
                        lane = lane_ref[tile, row, part]
                        got = [lane_take(table[c], lane) for c in range(2)]
                        real, imag = real_ref[tile, row, part], imag_ref[tile, row, part]
                        total[0][half] = total[0][half] + (got[0] * real - got[1] * imag)
                        total[1][half] = total[1][half] + (got[0] * imag + got[1] * real)
                sums += total[0] + total[1]
                if len(sums) == SUBLANES:
                    count = ((tile ^ near_ref[0]) * quarters + quarter) * (parts // halves) + block
                    out_ref[count // 2] = row_sums(sums)
                    sums = []


def swap(value, step):
    return lax.ppermute(value, "near", [(i, i ^ step) for i in range(SIDE)])


def local(profile, base_bin, tap_offset):
    pulses, pixels = base_bin.shape
    bins = profile.shape[2]
    each = pulses // SIDE
    quarters = SUBLANES // each
    length = pixels // quarters
    blocks, parts = length // BLOCK, length // LANES
    scale = 1.0 / math.sqrt(pulses * lax.axis_size(("x", "pair", "core")))
    vmem = pl.BlockSpec(memory_space=pltpu.VMEM)
    smem = pl.BlockSpec(memory_space=pltpu.SMEM)

    near = lax.axis_index("near").astype(jnp.int32).reshape(1)
    *index, shards = pl.pallas_call(
        arrange_kernel,
        out_shape=[jax.ShapeDtypeStruct((2, SUBLANES, length), jnp.int32)] * SIDE
        + [jax.ShapeDtypeStruct((SIDE * SIDE, 2, each, TAPS, bins // TAPS), jnp.float32)],
        in_specs=[smem] + [vmem] * 3,
        out_specs=[vmem] * (SIDE + 1),
        scratch_shapes=[pltpu.VMEM((2, pulses, TAPS, bins // TAPS), jnp.float32)],
        name="arrange",
    )(near, profile, base_bin, tap_offset)
    whole = lax.all_to_all(shards, ("far", "near"), 0, 0, tiled=True)
    index = jnp.stack([index[0]] + [swap(index[step], step) for step in range(1, SIDE)])
    by_part = (SIDE, SUBLANES, parts, TAPS, LANES)
    first, real, imag, lane = pl.pallas_call(
        lambda *refs: prepare_kernel(scale, *refs),
        out_shape=[
            jax.ShapeDtypeStruct((SIDE, SUBLANES, blocks), jnp.int32),
            jax.ShapeDtypeStruct(by_part, jnp.float32),
            jax.ShapeDtypeStruct(by_part, jnp.float32),
            jax.ShapeDtypeStruct(by_part, jnp.int32),
        ],
        in_specs=[vmem] * 2,
        out_specs=[vmem] * 4,
        cost_estimate=pl.CostEstimate(flops=pulses * pixels * 300, bytes_accessed=pulses * pixels * 104, transcendentals=0),
        compiler_params=pltpu.CompilerParams(vmem_limit_bytes=16 << 20),
        name="prepare",
    )(tap_table(), index)
    partial_image = pl.pallas_call(
        project_kernel,
        out_shape=jax.ShapeDtypeStruct((SIDE * pixels // BLOCK // 2, SUBLANES, LANES), jnp.float32),
        in_specs=[smem] * 2 + [vmem] * 4,
        out_specs=vmem,
        compiler_params=pltpu.CompilerParams(vmem_limit_bytes=24 << 20),
        name="project",
    )(near, first, whole, real, imag, lane)
    partial_image = partial_image.reshape(SIDE * pixels // BLOCK, 2 * BLOCK // LANES, LANES)
    received = lax.all_to_all(partial_image, ("near", "x", "pair", "core"), 0, 0, tiled=True)
    return jnp.sum(received, axis=0).reshape(2, BLOCK)


def solution(mesh):
    inner = Mesh(mesh.devices.reshape(SIZES), AXES)
    pulse, tile = ("x", "pair", "core"), ("far", "near")
    return jax.shard_map(
        local,
        mesh=inner,
        in_specs=(P(None, pulse, tile), P(pulse, tile), P(pulse, tile)),
        out_specs=P(None, tile + pulse),
        check_vma=False,
    )
```

```python
import math

import jax
import jax.numpy as jnp
from jax import lax
from jax.experimental import pallas as pl
from jax.experimental.pallas import tpu as pltpu
from jax.sharding import Mesh
from jax.sharding import PartitionSpec as P

TAPS = 8
FRAC = 16
BLOCK = 256
LANES = 128
SUBLANES = 8
SIDE = 4
AXES = ("far", "near", "x", "pair", "core")
SIZES = (4, 4, 4, 2, 2)


def tap_table():
    frac_part = jnp.arange(FRAC, dtype=jnp.float32)[:, None] / FRAC
    shift = jnp.arange(TAPS, dtype=jnp.float32)[None, :] - (TAPS // 2 - 1)
    offset = shift - frac_part
    values = jnp.sinc(offset) * (0.5 + 0.5 * jnp.cos(math.pi * offset / (TAPS // 2)))
    values = values / jnp.sum(values, axis=1, keepdims=True)
    return values.reshape(1, FRAC * TAPS)


def lane_take(row, index):
    return jnp.take_along_axis(row, index, axis=1, mode="promise_in_bounds")


def spread(row):
    return jnp.broadcast_to(row, (SUBLANES, LANES))


def cos_sin(steps):
    quarter = (steps + 512) >> 10
    x = (steps - (quarter << 10)).astype(jnp.float32) * (2.0 * math.pi / 4096.0)
    y = x * x
    s = x * (1.0 + y * (-1.0 / 6.0 + y * (1.0 / 120.0 + y * (-1.0 / 5040.0 + y * (1.0 / 362880.0)))))
    c = 1.0 + y * (-0.5 + y * (1.0 / 24.0 + y * (-1.0 / 720.0 + y * (1.0 / 40320.0))))
    odd = (quarter & 1) == 1
    cosine = jnp.where(odd, s, c)
    sine = jnp.where(odd, c, s)
    cosine = jnp.where(((quarter + 1) & 2) == 2, -cosine, cosine)
    sine = jnp.where((quarter & 2) == 2, -sine, sine)
    return cosine, sine


def arrange_kernel(shard_ref, bins_ref, offsets_ref, *refs):
    *index_refs, out_ref, tiles = refs
    near = lax.axis_index("near")
    lane = lax.broadcasted_iota(jnp.int32, (SUBLANES, LANES), 1)
    source = (lane & 15) * TAPS
    part = lane >> 4
    each = out_ref.shape[2]
    for c in range(2):
        rows = [shard_ref[c, :, t * LANES : (t + 1) * LANES] for t in range(TAPS)]
        for v in range(TAPS):
            got = lane_take(rows[0], source + v)
            for t in range(1, TAPS):
                got = jnp.where(part == t, lane_take(rows[t], source + v), got)
            tiles[c, :, v, :] = got
    quarters = SUBLANES // each
    length = index_refs[0].shape[2]
    for step, index_ref in enumerate(index_refs):
        for k, ref in enumerate((bins_ref, offsets_ref)):
            for p in range(each):
                pulse = pl.ds((near ^ step) * each + p, 1)
                for q in range(quarters):
                    row = p * quarters + q
                    index_ref[k, row : row + 1, :] = ref[pulse, q * length : (q + 1) * length]
    for c in range(2):
        for place in range(SIDE):
            for p in range(each):
                tile = tiles[c, place * each + p]
                for far in range(SIDE):
                    out_ref[far * SIDE + place, c, p] = tile


def prepare_kernel(scale, table_ref, index_ref, first_ref, real_ref, imag_ref, lane_ref):
    tiles, _, rows, length = index_ref.shape
    halves = BLOCK // LANES
    table = spread(table_ref[:, :])
    phase = lax.broadcasted_iota(jnp.int32, (SUBLANES, LANES), 0)
    for tile in range(tiles):
        for part in range(length // LANES):
            lanes = pl.ds(part * LANES, LANES)
            bins = index_ref[tile, 0, :, lanes]
            least = bins if part % halves == 0 else jnp.minimum(least, bins)
            if part % halves == halves - 1:
                block = part // halves
                lowest = jnp.min(least.astype(jnp.float32), axis=1, keepdims=True)
                count = tile * (length // BLOCK) + block
                first_ref[:, count : count + 1] = lowest.astype(jnp.int32)
            fine = bins * FRAC + index_ref[tile, 1, :, lanes]
            cosine, sine = cos_sin((fine * 2861) & 4095)
            cosine, sine = cosine * scale, sine * scale
            for s in range(rows):
                fine_s = spread(fine[s : s + 1])
                bins_s = fine_s >> 4
                weight = lane_take(table, ((fine_s & 15) << 3) + ((phase - bins_s) & 7))
                real_ref[tile, s, part] = weight * spread(cosine[s : s + 1])
                imag_ref[tile, s, part] = weight * spread(sine[s : s + 1])
                lane_ref[tile, s, part] = ((bins_s - phase + 7) >> 3) & (LANES - 1)


def row_sums(values):
    row = lax.broadcasted_iota(jnp.int32, (SUBLANES, LANES), 0)
    low = (row & 4) == 0
    values = [jnp.where(low, a, b) + pltpu.roll(jnp.where(low, b, a), 4, 0) for a, b in zip(values[:4], values[4:])]
    for step in (2, 1):
        low = (row & step) == 0
        values = [
            jnp.where(low, a + pltpu.roll(a, SUBLANES - step, 0), b + pltpu.roll(b, step, 0))
            for a, b in zip(values[:step], values[step:])
        ]
    return values[0]


def project_kernel(own, first_ref, whole, real_ref, imag_ref, lane_ref, out_ref):
    tiles, rows, parts = real_ref.shape[:3]
    owners, _, each = whole.shape[:3]
    quarters = rows // each
    halves = BLOCK // LANES
    near, core = lax.axis_index("near"), lax.axis_index("core")
    parity = core if own else 1 - core
    column = lax.broadcasted_iota(jnp.int32, (SUBLANES, LANES), 1)
    for tile in range(tiles):
        for quarter in range(quarters):
            sums = []
            for pair in range(parts // halves // 2):
                block = 2 * pair + parity
                total = [[jnp.zeros((SUBLANES, LANES), jnp.float32) for _ in range(halves)] for _ in range(2)]
                for p in range(each):
                    row = p * quarters + quarter
                    first = first_ref[row, tile * (parts // halves) + block]
                    owner = first >> 10
                    after = jnp.minimum(owner + 1, owners - 1)
                    here = column >= ((first >> 3) & (LANES - 1))
                    table = [jnp.where(here, whole[owner, c, p], whole[after, c, p]) for c in range(2)]
                    for half in range(halves):
                        part = block * halves + half
                        lane = lane_ref[tile, row, part]
                        got = [lane_take(table[c], lane) for c in range(2)]
                        real, imag = real_ref[tile, row, part], imag_ref[tile, row, part]
                        total[0][half] = total[0][half] + (got[0] * real - got[1] * imag)
                        total[1][half] = total[1][half] + (got[0] * imag + got[1] * real)
                sums += total[0] + total[1]
            out_ref[(tile ^ near) * quarters + quarter] = row_sums(sums)


def swap(value, step):
    return lax.ppermute(value, "near", [(i, i ^ step) for i in range(SIDE)])


def local(profile, base_bin, tap_offset):
    pulses, pixels = base_bin.shape
    bins = profile.shape[2]
    each = pulses // SIDE
    quarters = SUBLANES // each
    length = pixels // quarters
    blocks, parts = length // BLOCK, length // LANES
    scale = 1.0 / math.sqrt(pulses * lax.axis_size(("x", "pair", "core")))
    vmem = pl.BlockSpec(memory_space=pltpu.VMEM)
    smem = pl.BlockSpec(memory_space=pltpu.SMEM)

    *index, shards = pl.pallas_call(
        arrange_kernel,
        out_shape=[jax.ShapeDtypeStruct((2, SUBLANES, length), jnp.int32)] * SIDE
        + [jax.ShapeDtypeStruct((SIDE * SIDE, 2, each, TAPS, bins // TAPS), jnp.float32)],
        in_specs=[vmem] * 3,
        out_specs=[vmem] * (SIDE + 1),
        scratch_shapes=[pltpu.VMEM((2, pulses, TAPS, bins // TAPS), jnp.float32)],
        name="arrange",
    )(profile, base_bin, tap_offset)
    whole = lax.all_to_all(shards, ("far", "near"), 0, 0, tiled=True)
    index = jnp.stack([index[0]] + [swap(index[step], step) for step in range(1, SIDE)])
    by_part = (SIDE, SUBLANES, parts, TAPS, LANES)
    first, real, imag, lane = pl.pallas_call(
        lambda *refs: prepare_kernel(scale, *refs),
        out_shape=[
            jax.ShapeDtypeStruct((SUBLANES, SIDE * blocks), jnp.int32),
            jax.ShapeDtypeStruct(by_part, jnp.float32),
            jax.ShapeDtypeStruct(by_part, jnp.float32),
            jax.ShapeDtypeStruct(by_part, jnp.int32),
        ],
        in_specs=[vmem] * 2,
        out_specs=[vmem] * 4,
        cost_estimate=pl.CostEstimate(flops=pulses * pixels * 300, bytes_accessed=pulses * pixels * 104, transcendentals=0),
        compiler_params=pltpu.CompilerParams(vmem_limit_bytes=16 << 20),
        name="prepare",
    )(tap_table(), index)
    def project(own):
        return pl.pallas_call(
            lambda *refs: project_kernel(own, *refs),
            out_shape=jax.ShapeDtypeStruct((SIDE * quarters, SUBLANES, LANES), jnp.float32),
            in_specs=[smem] + [vmem] * 4,
            out_specs=vmem,
            cost_estimate=pl.CostEstimate(flops=1 << 24, bytes_accessed=2 << 20, transcendentals=0),
            compiler_params=pltpu.CompilerParams(vmem_limit_bytes=24 << 20),
            name="project",
        )(first, whole, real, imag, lane)

    theirs = lax.ppermute(project(False), "core", [(0, 1), (1, 0)])
    partial_image = (project(True) + theirs).reshape(SIDE * pixels // BLOCK // 2, 2 * BLOCK // LANES, LANES)
    received = lax.all_to_all(partial_image, ("near", "x", "pair"), 0, 0, tiled=True)
    return jnp.sum(received, axis=0).reshape(2, BLOCK)


def solution(mesh):
    inner = Mesh(mesh.devices.reshape(SIZES), AXES)
    pulse, tile = ("x", "pair", "core"), ("far", "near")
    return jax.shard_map(
        local,
        mesh=inner,
        in_specs=(P(None, pulse, tile), P(pulse, tile), P(pulse, tile)),
        out_specs=P(None, tile + pulse),
        check_vma=False,
    )
```

```python
import math

import jax
import jax.numpy as jnp
from jax import lax
from jax.experimental import pallas as pl
from jax.experimental.pallas import tpu as pltpu
from jax.sharding import Mesh
from jax.sharding import PartitionSpec as P

TAPS = 8
FRAC = 16
BLOCK = 256
LANES = 128
SUBLANES = 8
SIDE = 4
AXES = ("far", "near", "x", "pair", "core")
SIZES = (4, 4, 4, 2, 2)


def tap_table():
    frac_part = jnp.arange(FRAC, dtype=jnp.float32)[:, None] / FRAC
    shift = jnp.arange(TAPS, dtype=jnp.float32)[None, :] - (TAPS // 2 - 1)
    offset = shift - frac_part
    values = jnp.sinc(offset) * (0.5 + 0.5 * jnp.cos(math.pi * offset / (TAPS // 2)))
    values = values / jnp.sum(values, axis=1, keepdims=True)
    return values.reshape(1, FRAC * TAPS)


def lane_take(row, index):
    return jnp.take_along_axis(row, index, axis=1, mode="promise_in_bounds")


def spread(row):
    return jnp.broadcast_to(row, (SUBLANES, LANES))


def cos_sin(steps):
    quarter = (steps + 512) >> 10
    x = (steps - (quarter << 10)).astype(jnp.float32) * (2.0 * math.pi / 4096.0)
    y = x * x
    s = x * (1.0 + y * (-1.0 / 6.0 + y * (1.0 / 120.0 + y * (-1.0 / 5040.0 + y * (1.0 / 362880.0)))))
    c = 1.0 + y * (-0.5 + y * (1.0 / 24.0 + y * (-1.0 / 720.0 + y * (1.0 / 40320.0))))
    odd = (quarter & 1) == 1
    cosine = jnp.where(odd, s, c)
    sine = jnp.where(odd, c, s)
    cosine = jnp.where(((quarter + 1) & 2) == 2, -cosine, cosine)
    sine = jnp.where((quarter & 2) == 2, -sine, sine)
    return cosine, sine


def arrange_kernel(shard_ref, bins_ref, offsets_ref, *refs):
    *index_refs, out_ref, tiles = refs
    near = lax.axis_index("near")
    lane = lax.broadcasted_iota(jnp.int32, (SUBLANES, LANES), 1)
    source = (lane & 15) * TAPS
    part = lane >> 4
    each = out_ref.shape[2]
    for c in range(2):
        rows = [shard_ref[c, :, t * LANES : (t + 1) * LANES] for t in range(TAPS)]
        for v in range(TAPS):
            got = lane_take(rows[0], source + v)
            for t in range(1, TAPS):
                got = jnp.where(part == t, lane_take(rows[t], source + v), got)
            tiles[c, :, v, :] = got
    quarters = SUBLANES // each
    length = index_refs[0].shape[2]
    for step, index_ref in enumerate(index_refs):
        for k, ref in enumerate((bins_ref, offsets_ref)):
            for p in range(each):
                pulse = pl.ds((near ^ step) * each + p, 1)
                for q in range(quarters):
                    row = p * quarters + q
                    index_ref[k, row : row + 1, :] = ref[pulse, q * length : (q + 1) * length]
    for c in range(2):
        for place in range(SIDE):
            for p in range(each):
                tile = tiles[c, place * each + p]
                for far in range(SIDE):
                    out_ref[far * SIDE + place, c, p] = tile


def prepare_kernel(scale, table_ref, index_ref, first_ref, real_ref, imag_ref, lane_ref, lowest_ref, sem):
    tiles, _, rows, length = index_ref.shape
    halves = BLOCK // LANES
    table = spread(table_ref[:, :])
    phase = lax.broadcasted_iota(jnp.int32, (SUBLANES, LANES), 0)
    lowest_ref[:, :] = jnp.zeros(lowest_ref.shape, jnp.int32)
    for tile in range(tiles):
        for block in range(length // BLOCK):
            pair = [index_ref[tile, 0, :, (block * halves + h) * LANES : (block * halves + h + 1) * LANES] for h in range(halves)]
            lowest = jnp.min(jnp.minimum(*pair).astype(jnp.float32), axis=1, keepdims=True)
            count = tile * (length // BLOCK) + block
            lowest_ref[:, count : count + 1] = lowest.astype(jnp.int32)
    copy = pltpu.make_async_copy(lowest_ref, first_ref, sem)
    copy.start()
    for tile in range(tiles):
        for part in range(length // LANES):
            lanes = pl.ds(part * LANES, LANES)
            fine = index_ref[tile, 0, :, lanes] * FRAC + index_ref[tile, 1, :, lanes]
            cosine, sine = cos_sin((fine * 2861) & 4095)
            cosine, sine = cosine * scale, sine * scale
            for s in range(rows):
                fine_s = spread(fine[s : s + 1])
                bins_s = fine_s >> 4
                weight = lane_take(table, ((fine_s & 15) << 3) + ((phase - bins_s) & 7))
                real_ref[tile, s, part] = weight * spread(cosine[s : s + 1])
                imag_ref[tile, s, part] = weight * spread(sine[s : s + 1])
                lane_ref[tile, s, part] = ((bins_s - phase + 7) >> 3) & (LANES - 1)
    copy.wait()


def row_sums(values):
    row = lax.broadcasted_iota(jnp.int32, (SUBLANES, LANES), 0)
    low = (row & 4) == 0
    values = [jnp.where(low, a, b) + pltpu.roll(jnp.where(low, b, a), 4, 0) for a, b in zip(values[:4], values[4:])]
    for step in (2, 1):
        low = (row & step) == 0
        values = [
            jnp.where(low, a + pltpu.roll(a, SUBLANES - step, 0), b + pltpu.roll(b, step, 0))
            for a, b in zip(values[:step], values[step:])
        ]
    return values[0]


def project_kernel(own, first_ref, whole, real_ref, imag_ref, lane_ref, out_ref):
    tiles, rows, parts = real_ref.shape[:3]
    owners, _, each = whole.shape[:3]
    quarters = rows // each
    halves = BLOCK // LANES
    near, core = lax.axis_index("near"), lax.axis_index("core")
    parity = core if own else 1 - core
    column = lax.broadcasted_iota(jnp.int32, (SUBLANES, LANES), 1)
    for tile in range(tiles):
        for quarter in range(quarters):
            sums = []
            for pair in range(parts // halves // 2):
                block = 2 * pair + parity
                total = [[jnp.zeros((SUBLANES, LANES), jnp.float32) for _ in range(halves)] for _ in range(2)]
                for p in range(each):
                    row = p * quarters + quarter
                    first = first_ref[row, tile * (parts // halves) + block]
                    owner = first >> 10
                    after = jnp.minimum(owner + 1, owners - 1)
                    here = column >= ((first >> 3) & (LANES - 1))
                    table = [jnp.where(here, whole[owner, c, p], whole[after, c, p]) for c in range(2)]
                    for half in range(halves):
                        part = block * halves + half
                        lane = lane_ref[tile, row, part]
                        got = [lane_take(table[c], lane) for c in range(2)]
                        real, imag = real_ref[tile, row, part], imag_ref[tile, row, part]
                        total[0][half] = total[0][half] + (got[0] * real - got[1] * imag)
                        total[1][half] = total[1][half] + (got[0] * imag + got[1] * real)
                sums += total[0] + total[1]
            out_ref[(tile ^ near) * quarters + quarter] = row_sums(sums)


def swap(value, step):
    return lax.ppermute(value, "near", [(i, i ^ step) for i in range(SIDE)])


def local(profile, base_bin, tap_offset):
    pulses, pixels = base_bin.shape
    bins = profile.shape[2]
    each = pulses // SIDE
    quarters = SUBLANES // each
    length = pixels // quarters
    blocks, parts = length // BLOCK, length // LANES
    scale = 1.0 / math.sqrt(pulses * lax.axis_size(("x", "pair", "core")))
    vmem = pl.BlockSpec(memory_space=pltpu.VMEM)
    smem = pl.BlockSpec(memory_space=pltpu.SMEM)

    *index, shards = pl.pallas_call(
        arrange_kernel,
        out_shape=[jax.ShapeDtypeStruct((2, SUBLANES, length), jnp.int32)] * SIDE
        + [jax.ShapeDtypeStruct((SIDE * SIDE, 2, each, TAPS, bins // TAPS), jnp.float32)],
        in_specs=[vmem] * 3,
        out_specs=[vmem] * (SIDE + 1),
        scratch_shapes=[pltpu.VMEM((2, pulses, TAPS, bins // TAPS), jnp.float32)],
        name="arrange",
    )(profile, base_bin, tap_offset)
    whole = lax.all_to_all(shards, ("far", "near"), 0, 0, tiled=True)
    index = jnp.stack([index[0]] + [swap(index[step], step) for step in range(1, SIDE)])
    by_part = (SIDE, SUBLANES, parts, TAPS, LANES)
    first, real, imag, lane = pl.pallas_call(
        lambda *refs: prepare_kernel(scale, *refs),
        out_shape=[
            pltpu.SMEM((SUBLANES, LANES), jnp.int32),
            jax.ShapeDtypeStruct(by_part, jnp.float32),
            jax.ShapeDtypeStruct(by_part, jnp.float32),
            jax.ShapeDtypeStruct(by_part, jnp.int32),
        ],
        in_specs=[vmem] * 2,
        out_specs=[smem] + [vmem] * 3,
        scratch_shapes=[pltpu.VMEM((SUBLANES, LANES), jnp.int32), pltpu.SemaphoreType.DMA],
        cost_estimate=pl.CostEstimate(flops=pulses * pixels * 300, bytes_accessed=pulses * pixels * 104, transcendentals=0),
        compiler_params=pltpu.CompilerParams(vmem_limit_bytes=16 << 20),
        name="prepare",
    )(tap_table(), index)
    def project(own):
        return pl.pallas_call(
            lambda *refs: project_kernel(own, *refs),
            out_shape=jax.ShapeDtypeStruct((SIDE * quarters, SUBLANES, LANES), jnp.float32),
            in_specs=[smem] + [vmem] * 4,
            out_specs=vmem,
            cost_estimate=pl.CostEstimate(flops=1 << 24, bytes_accessed=2 << 20, transcendentals=0),
            compiler_params=pltpu.CompilerParams(vmem_limit_bytes=24 << 20),
            name="project",
        )(first, whole, real, imag, lane)

    theirs = lax.ppermute(project(False), "core", [(0, 1), (1, 0)])
    partial_image = (project(True) + theirs).reshape(SIDE * pixels // BLOCK // 2, 2 * BLOCK // LANES, LANES)
    received = lax.all_to_all(partial_image, ("near", "x", "pair"), 0, 0, tiled=True)
    return jnp.sum(received, axis=0).reshape(2, BLOCK)


def solution(mesh):
    inner = Mesh(mesh.devices.reshape(SIZES), AXES)
    pulse, tile = ("x", "pair", "core"), ("far", "near")
    return jax.shard_map(
        local,
        mesh=inner,
        in_specs=(P(None, pulse, tile), P(pulse, tile), P(pulse, tile)),
        out_specs=P(None, tile + pulse),
        check_vma=False,
    )
```

```python
import math

import jax
import jax.numpy as jnp
from jax import lax
from jax.experimental import pallas as pl
from jax.experimental.pallas import tpu as pltpu
from jax.sharding import Mesh
from jax.sharding import PartitionSpec as P

TAPS = 8
FRAC = 16
BLOCK = 256
LANES = 128
SUBLANES = 8
SIDE = 4
AXES = ("far", "near", "x", "pair", "core")
SIZES = (4, 4, 4, 2, 2)


def tap_table():
    frac_part = jnp.arange(FRAC, dtype=jnp.float32)[:, None] / FRAC
    shift = jnp.arange(TAPS, dtype=jnp.float32)[None, :] - (TAPS // 2 - 1)
    offset = shift - frac_part
    values = jnp.sinc(offset) * (0.5 + 0.5 * jnp.cos(math.pi * offset / (TAPS // 2)))
    values = values / jnp.sum(values, axis=1, keepdims=True)
    return values.reshape(1, FRAC * TAPS)


def lane_take(row, index):
    return jnp.take_along_axis(row, index, axis=1, mode="promise_in_bounds")


def spread(row):
    return jnp.broadcast_to(row, (SUBLANES, LANES))


def cos_sin(steps):
    quarter = (steps + 512) >> 10
    x = (steps - (quarter << 10)).astype(jnp.float32) * (2.0 * math.pi / 4096.0)
    y = x * x
    s = x * (1.0 + y * (-1.0 / 6.0 + y * (1.0 / 120.0 + y * (-1.0 / 5040.0 + y * (1.0 / 362880.0)))))
    c = 1.0 + y * (-0.5 + y * (1.0 / 24.0 + y * (-1.0 / 720.0 + y * (1.0 / 40320.0))))
    odd = (quarter & 1) == 1
    cosine = jnp.where(odd, s, c)
    sine = jnp.where(odd, c, s)
    cosine = jnp.where(((quarter + 1) & 2) == 2, -cosine, cosine)
    sine = jnp.where((quarter & 2) == 2, -sine, sine)
    return cosine, sine


def arrange_kernel(shard_ref, bins_ref, offsets_ref, *refs):
    *index_refs, out_ref, tiles = refs
    near = lax.axis_index("near")
    lane = lax.broadcasted_iota(jnp.int32, (SUBLANES, LANES), 1)
    source = (lane & 15) * TAPS
    part = lane >> 4
    each = out_ref.shape[2]
    for c in range(2):
        rows = [shard_ref[c, :, t * LANES : (t + 1) * LANES] for t in range(TAPS)]
        for v in range(TAPS):
            got = lane_take(rows[0], source + v)
            for t in range(1, TAPS):
                got = jnp.where(part == t, lane_take(rows[t], source + v), got)
            tiles[c, :, v, :] = got
    quarters = SUBLANES // each
    length = index_refs[0].shape[2]
    for step, index_ref in enumerate(index_refs):
        for k, ref in enumerate((bins_ref, offsets_ref)):
            for p in range(each):
                pulse = pl.ds((near ^ step) * each + p, 1)
                for q in range(quarters):
                    row = p * quarters + q
                    index_ref[k, row : row + 1, :] = ref[pulse, q * length : (q + 1) * length]
    for c in range(2):
        for place in range(SIDE):
            for p in range(each):
                tile = tiles[c, place * each + p]
                for far in range(SIDE):
                    out_ref[far * SIDE + place, c, p] = tile


def prepare_kernel(scale, table_ref, index_ref, first_ref, real_ref, imag_ref, lane_ref, lowest_ref, sem):
    tiles, _, rows, length = index_ref.shape
    halves = BLOCK // LANES
    table = spread(table_ref[:, :])
    phase = lax.broadcasted_iota(jnp.int32, (SUBLANES, LANES), 0)
    lowest_ref[:, :] = jnp.zeros(lowest_ref.shape, jnp.int32)
    for tile in range(tiles):
        for block in range(length // BLOCK):
            pair = [index_ref[tile, 0, :, (block * halves + h) * LANES : (block * halves + h + 1) * LANES] for h in range(halves)]
            lowest = jnp.min(jnp.minimum(*pair).astype(jnp.float32), axis=1, keepdims=True)
            count = tile * (length // BLOCK) + block
            lowest_ref[:, count : count + 1] = lowest.astype(jnp.int32)
    copy = pltpu.make_async_copy(lowest_ref, first_ref, sem)
    copy.start()
    for tile in range(tiles):
        for part in range(length // LANES):
            lanes = pl.ds(part * LANES, LANES)
            fine = index_ref[tile, 0, :, lanes] * FRAC + index_ref[tile, 1, :, lanes]
            cosine, sine = cos_sin((fine * 2861) & 4095)
            cosine, sine = cosine * scale, sine * scale
            for s in range(rows):
                fine_s = spread(fine[s : s + 1])
                bins_s = fine_s >> 4
                weight = lane_take(table, ((fine_s & 15) << 3) + ((phase - bins_s) & 7))
                real_ref[tile, s, part] = weight * spread(cosine[s : s + 1])
                imag_ref[tile, s, part] = weight * spread(sine[s : s + 1])
                lane_ref[tile, s, part] = ((bins_s - phase + 7) >> 3) & (LANES - 1)
    copy.wait()


def row_sums(values):
    row = lax.broadcasted_iota(jnp.int32, (SUBLANES, LANES), 0)
    low = (row & 4) == 0
    values = [jnp.where(low, a, b) + pltpu.roll(jnp.where(low, b, a), 4, 0) for a, b in zip(values[:4], values[4:])]
    for step in (2, 1):
        low = (row & step) == 0
        values = [
            jnp.where(low, a + pltpu.roll(a, SUBLANES - step, 0), b + pltpu.roll(b, step, 0))
            for a, b in zip(values[:step], values[step:])
        ]
    return values[0]


def project_kernel(own, first_ref, whole, real_ref, imag_ref, lane_ref, out_ref):
    tiles, rows, parts = real_ref.shape[:3]
    owners, _, each = whole.shape[:3]
    quarters = rows // each
    halves = BLOCK // LANES
    near, core = lax.axis_index("near"), lax.axis_index("core")
    parity = core if own else 1 - core
    column = lax.broadcasted_iota(jnp.int32, (SUBLANES, LANES), 1)
    for tile in range(tiles):
        for quarter in range(quarters):
            sums = []
            for pair in range(parts // halves // 2):
                block = 2 * pair + parity
                total = [[jnp.zeros((SUBLANES, LANES), jnp.float32) for _ in range(halves)] for _ in range(2)]
                for p in range(each):
                    row = p * quarters + quarter
                    first = first_ref[row, tile * (parts // halves) + block]
                    owner = first >> 10
                    after = jnp.minimum(owner + 1, owners - 1)
                    here = column >= ((first >> 3) & (LANES - 1))
                    table = [jnp.where(here, whole[owner, c, p], whole[after, c, p]) for c in range(2)]
                    for half in range(halves):
                        part = block * halves + half
                        lane = lane_ref[tile, row, part]
                        got = [lane_take(table[c], lane) for c in range(2)]
                        real, imag = real_ref[tile, row, part], imag_ref[tile, row, part]
                        total[0][half] = total[0][half] + (got[0] * real - got[1] * imag)
                        total[1][half] = total[1][half] + (got[0] * imag + got[1] * real)
                sums += total[0] + total[1]
            out_ref[(tile ^ near) * quarters + quarter] = row_sums(sums)


def swap(value, step):
    return lax.ppermute(value, "near", [(i, i ^ step) for i in range(SIDE)])


def local(profile, base_bin, tap_offset):
    pulses, pixels = base_bin.shape
    bins = profile.shape[2]
    each = pulses // SIDE
    quarters = SUBLANES // each
    length = pixels // quarters
    blocks, parts = length // BLOCK, length // LANES
    scale = 1.0 / math.sqrt(pulses * lax.axis_size(("x", "pair", "core")))
    vmem = pl.BlockSpec(memory_space=pltpu.VMEM)
    smem = pl.BlockSpec(memory_space=pltpu.SMEM)

    *index, shards = pl.pallas_call(
        arrange_kernel,
        out_shape=[jax.ShapeDtypeStruct((2, SUBLANES, length), jnp.int32)] * SIDE
        + [jax.ShapeDtypeStruct((SIDE * SIDE, 2, each, TAPS, bins // TAPS), jnp.float32)],
        in_specs=[vmem] * 3,
        out_specs=[vmem] * (SIDE + 1),
        scratch_shapes=[pltpu.VMEM((2, pulses, TAPS, bins // TAPS), jnp.float32)],
        compiler_params=pltpu.CompilerParams(vmem_limit_bytes=4 << 20),
        name="arrange",
    )(*(pltpu.with_memory_space_constraint(value, pltpu.HBM) for value in (profile, base_bin, tap_offset)))
    whole = lax.all_to_all(shards, ("far", "near"), 0, 0, tiled=True)
    index = jnp.stack([index[0]] + [swap(index[step], step) for step in range(1, SIDE)])
    by_part = (SIDE, SUBLANES, parts, TAPS, LANES)
    first, real, imag, lane = pl.pallas_call(
        lambda *refs: prepare_kernel(scale, *refs),
        out_shape=[
            pltpu.SMEM((SUBLANES, LANES), jnp.int32),
            jax.ShapeDtypeStruct(by_part, jnp.float32),
            jax.ShapeDtypeStruct(by_part, jnp.float32),
            jax.ShapeDtypeStruct(by_part, jnp.int32),
        ],
        in_specs=[vmem] * 2,
        out_specs=[smem] + [vmem] * 3,
        scratch_shapes=[pltpu.VMEM((SUBLANES, LANES), jnp.int32), pltpu.SemaphoreType.DMA],
        cost_estimate=pl.CostEstimate(flops=pulses * pixels * 300, bytes_accessed=pulses * pixels * 104, transcendentals=0),
        compiler_params=pltpu.CompilerParams(vmem_limit_bytes=16 << 20),
        name="prepare",
    )(tap_table(), index)
    def project(own):
        return pl.pallas_call(
            lambda *refs: project_kernel(own, *refs),
            out_shape=jax.ShapeDtypeStruct((SIDE * quarters, SUBLANES, LANES), jnp.float32),
            in_specs=[smem] + [vmem] * 4,
            out_specs=vmem,
            cost_estimate=pl.CostEstimate(flops=1 << 24, bytes_accessed=2 << 20, transcendentals=0),
            compiler_params=pltpu.CompilerParams(vmem_limit_bytes=24 << 20),
            name="project",
        )(first, whole, real, imag, lane)

    theirs = lax.ppermute(project(False), "core", [(0, 1), (1, 0)])
    partial_image = (project(True) + theirs).reshape(SIDE * pixels // BLOCK // 2, 2 * BLOCK // LANES, LANES)
    received = lax.all_to_all(partial_image, ("near", "x", "pair"), 0, 0, tiled=True)
    return jnp.sum(received, axis=0).reshape(2, BLOCK)


def solution(mesh):
    inner = Mesh(mesh.devices.reshape(SIZES), AXES)
    pulse, tile = ("x", "pair", "core"), ("far", "near")
    return jax.shard_map(
        local,
        mesh=inner,
        in_specs=(P(None, pulse, tile), P(pulse, tile), P(pulse, tile)),
        out_specs=P(None, tile + pulse),
        check_vma=False,
    )
```

```python
import math

import jax
import jax.numpy as jnp
from jax import lax
from jax.experimental import pallas as pl
from jax.experimental.pallas import tpu as pltpu
from jax.sharding import Mesh
from jax.sharding import PartitionSpec as P

TAPS = 8
FRAC = 16
BLOCK = 256
LANES = 128
SUBLANES = 8
SIDE = 4
AXES = ("far", "near", "x", "pair", "core")
SIZES = (4, 4, 4, 2, 2)


def tap_table():
    frac_part = jnp.arange(FRAC, dtype=jnp.float32)[:, None] / FRAC
    shift = jnp.arange(TAPS, dtype=jnp.float32)[None, :] - (TAPS // 2 - 1)
    offset = shift - frac_part
    values = jnp.sinc(offset) * (0.5 + 0.5 * jnp.cos(math.pi * offset / (TAPS // 2)))
    values = values / jnp.sum(values, axis=1, keepdims=True)
    return values.reshape(1, FRAC * TAPS)


def lane_take(row, index):
    return jnp.take_along_axis(row, index, axis=1, mode="promise_in_bounds")


def spread(row):
    return jnp.broadcast_to(row, (SUBLANES, LANES))


def cos_sin(steps):
    quarter = (steps + 512) >> 10
    x = (steps - (quarter << 10)).astype(jnp.float32) * (2.0 * math.pi / 4096.0)
    y = x * x
    s = x * (1.0 + y * (-1.0 / 6.0 + y * (1.0 / 120.0 + y * (-1.0 / 5040.0 + y * (1.0 / 362880.0)))))
    c = 1.0 + y * (-0.5 + y * (1.0 / 24.0 + y * (-1.0 / 720.0 + y * (1.0 / 40320.0))))
    odd = (quarter & 1) == 1
    cosine = jnp.where(odd, s, c)
    sine = jnp.where(odd, c, s)
    cosine = jnp.where(((quarter + 1) & 2) == 2, -cosine, cosine)
    sine = jnp.where((quarter & 2) == 2, -sine, sine)
    return cosine, sine


def arrange_kernel(shard_ref, bins_ref, offsets_ref, *refs):
    *index_refs, out_ref, tiles = refs
    near = lax.axis_index("near")
    lane = lax.broadcasted_iota(jnp.int32, (SUBLANES, LANES), 1)
    source = (lane & 15) * TAPS
    part = lane >> 4
    each = out_ref.shape[2]
    for c in range(2):
        rows = [shard_ref[c, :, t * LANES : (t + 1) * LANES] for t in range(TAPS)]
        for v in range(TAPS):
            got = lane_take(rows[0], source + v)
            for t in range(1, TAPS):
                got = jnp.where(part == t, lane_take(rows[t], source + v), got)
            tiles[c, :, v, :] = got
    quarters = SUBLANES // each
    length = index_refs[0].shape[2]
    for step, index_ref in enumerate(index_refs):
        for k, ref in enumerate((bins_ref, offsets_ref)):
            for p in range(each):
                pulse = pl.ds((near ^ step) * each + p, 1)
                for q in range(quarters):
                    row = p * quarters + q
                    index_ref[k, row : row + 1, :] = ref[pulse, q * length : (q + 1) * length]
    for c in range(2):
        for place in range(SIDE):
            for p in range(each):
                tile = tiles[c, place * each + p]
                for far in range(SIDE):
                    out_ref[SIDE * SIDE - 1 - (far * SIDE + place), c, p] = tile


def prepare_kernel(scale, table_ref, index_ref, first_ref, real_ref, imag_ref, lane_ref, lowest_ref, sem):
    tiles, _, rows, length = index_ref.shape
    halves = BLOCK // LANES
    table = spread(table_ref[:, :])
    phase = lax.broadcasted_iota(jnp.int32, (SUBLANES, LANES), 0)
    lowest_ref[:, :] = jnp.zeros(lowest_ref.shape, jnp.int32)
    for tile in range(tiles):
        for block in range(length // BLOCK):
            pair = [index_ref[tile, 0, :, (block * halves + h) * LANES : (block * halves + h + 1) * LANES] for h in range(halves)]
            lowest = jnp.min(jnp.minimum(*pair).astype(jnp.float32), axis=1, keepdims=True)
            count = tile * (length // BLOCK) + block
            lowest_ref[:, count : count + 1] = lowest.astype(jnp.int32)
    copy = pltpu.make_async_copy(lowest_ref, first_ref, sem)
    copy.start()
    for tile in range(tiles):
        for part in range(length // LANES):
            lanes = pl.ds(part * LANES, LANES)
            fine = index_ref[tile, 0, :, lanes] * FRAC + index_ref[tile, 1, :, lanes]
            cosine, sine = cos_sin((fine * 2861) & 4095)
            cosine, sine = cosine * scale, sine * scale
            for s in range(rows):
                fine_s = spread(fine[s : s + 1])
                bins_s = fine_s >> 4
                weight = lane_take(table, ((fine_s & 15) << 3) + ((phase - bins_s) & 7))
                real_ref[tile, s, part] = weight * spread(cosine[s : s + 1])
                imag_ref[tile, s, part] = weight * spread(sine[s : s + 1])
                lane_ref[tile, s, part] = ((bins_s - phase + 7) >> 3) & (LANES - 1)
    copy.wait()


def row_sums(values):
    row = lax.broadcasted_iota(jnp.int32, (SUBLANES, LANES), 0)
    low = (row & 4) == 0
    values = [jnp.where(low, a, b) + pltpu.roll(jnp.where(low, b, a), 4, 0) for a, b in zip(values[:4], values[4:])]
    for step in (2, 1):
        low = (row & step) == 0
        values = [
            jnp.where(low, a + pltpu.roll(a, SUBLANES - step, 0), b + pltpu.roll(b, step, 0))
            for a, b in zip(values[:step], values[step:])
        ]
    return values[0]


def project_kernel(own, first_ref, whole, real_ref, imag_ref, lane_ref, out_ref):
    tiles, rows, parts = real_ref.shape[:3]
    owners, _, each = whole.shape[:3]
    quarters = rows // each
    halves = BLOCK // LANES
    near, core = lax.axis_index("near"), lax.axis_index("core")
    parity = core if own else 1 - core
    column = lax.broadcasted_iota(jnp.int32, (SUBLANES, LANES), 1)
    for tile in range(tiles):
        for quarter in range(quarters):
            sums = []
            for pair in range(parts // halves // 2):
                block = 2 * pair + parity
                total = [[jnp.zeros((SUBLANES, LANES), jnp.float32) for _ in range(halves)] for _ in range(2)]
                for p in range(each):
                    row = p * quarters + quarter
                    first = first_ref[row, tile * (parts // halves) + block]
                    owner = first >> 10
                    after = jnp.minimum(owner + 1, owners - 1)
                    here = column >= ((first >> 3) & (LANES - 1))
                    table = [jnp.where(here, whole[owners - 1 - owner, c, p], whole[owners - 1 - after, c, p]) for c in range(2)]
                    for half in range(halves):
                        part = block * halves + half
                        lane = lane_ref[tile, row, part]
                        got = [lane_take(table[c], lane) for c in range(2)]
                        real, imag = real_ref[tile, row, part], imag_ref[tile, row, part]
                        total[0][half] = total[0][half] + (got[0] * real - got[1] * imag)
                        total[1][half] = total[1][half] + (got[0] * imag + got[1] * real)
                sums = total[0] + total[1] + sums
            out_ref[tiles * quarters - 1 - ((tile ^ near) * quarters + quarter)] = row_sums(sums)


def swap(value, step):
    return lax.ppermute(value, "near", [(i, i ^ step) for i in range(SIDE)])


def backward(value, axes):
    return lax.all_to_all(value, axes, 0, 0, tiled=True, axis_index_groups=[list(range(value.shape[0]))[::-1]])


def local(profile, base_bin, tap_offset):
    pulses, pixels = base_bin.shape
    bins = profile.shape[2]
    each = pulses // SIDE
    quarters = SUBLANES // each
    length = pixels // quarters
    blocks, parts = length // BLOCK, length // LANES
    scale = 1.0 / math.sqrt(pulses * lax.axis_size(("x", "pair", "core")))
    vmem = pl.BlockSpec(memory_space=pltpu.VMEM)
    smem = pl.BlockSpec(memory_space=pltpu.SMEM)

    *index, shards = pl.pallas_call(
        arrange_kernel,
        out_shape=[jax.ShapeDtypeStruct((2, SUBLANES, length), jnp.int32)] * SIDE
        + [jax.ShapeDtypeStruct((SIDE * SIDE, 2, each, TAPS, bins // TAPS), jnp.float32)],
        in_specs=[vmem] * 3,
        out_specs=[vmem] * (SIDE + 1),
        scratch_shapes=[pltpu.VMEM((2, pulses, TAPS, bins // TAPS), jnp.float32)],
        compiler_params=pltpu.CompilerParams(vmem_limit_bytes=4 << 20),
        name="arrange",
    )(*(pltpu.with_memory_space_constraint(value, pltpu.HBM) for value in (profile, base_bin, tap_offset)))
    whole = backward(shards, ("far", "near"))
    index = jnp.stack([index[0]] + [swap(index[step], step) for step in range(1, SIDE)])
    by_part = (SIDE, SUBLANES, parts, TAPS, LANES)
    first, real, imag, lane = pl.pallas_call(
        lambda *refs: prepare_kernel(scale, *refs),
        out_shape=[
            pltpu.SMEM((SUBLANES, LANES), jnp.int32),
            jax.ShapeDtypeStruct(by_part, jnp.float32),
            jax.ShapeDtypeStruct(by_part, jnp.float32),
            jax.ShapeDtypeStruct(by_part, jnp.int32),
        ],
        in_specs=[vmem] * 2,
        out_specs=[smem] + [vmem] * 3,
        scratch_shapes=[pltpu.VMEM((SUBLANES, LANES), jnp.int32), pltpu.SemaphoreType.DMA],
        cost_estimate=pl.CostEstimate(flops=pulses * pixels * 300, bytes_accessed=pulses * pixels * 104, transcendentals=0),
        compiler_params=pltpu.CompilerParams(vmem_limit_bytes=16 << 20),
        name="prepare",
    )(tap_table(), index)
    def project(own):
        return pl.pallas_call(
            lambda *refs: project_kernel(own, *refs),
            out_shape=jax.ShapeDtypeStruct((SIDE * quarters, SUBLANES, LANES), jnp.float32),
            in_specs=[smem] + [vmem] * 4,
            out_specs=vmem,
            cost_estimate=pl.CostEstimate(flops=1 << 24, bytes_accessed=2 << 20, transcendentals=0),
            compiler_params=pltpu.CompilerParams(vmem_limit_bytes=24 << 20),
            name="project",
        )(first, whole, real, imag, lane)

    theirs = lax.ppermute(project(False), "core", [(0, 1), (1, 0)])
    partial_image = (project(True) + theirs).reshape(SIDE * pixels // BLOCK // 2, 2 * BLOCK // LANES, LANES)
    received = backward(partial_image, ("near", "x", "pair"))
    return jnp.sum(received, axis=0).reshape(2, BLOCK)


def solution(mesh):
    inner = Mesh(mesh.devices.reshape(SIZES), AXES)
    pulse, tile = ("x", "pair", "core"), ("far", "near")
    return jax.shard_map(
        local,
        mesh=inner,
        in_specs=(P(None, pulse, tile), P(pulse, tile), P(pulse, tile)),
        out_specs=P(None, tile + pulse),
        check_vma=False,
    )
```

```python
import math

import jax
import jax.numpy as jnp
from jax import lax
from jax.experimental import pallas as pl
from jax.experimental.pallas import tpu as pltpu
from jax.sharding import Mesh
from jax.sharding import PartitionSpec as P

TAPS = 8
FRAC = 16
BLOCK = 256
LANES = 128
SUBLANES = 8
SIDE = 4
STEPS = (0, 3, 2, 1)
AXES = ("far", "near", "x", "pair", "core")
SIZES = (4, 4, 4, 2, 2)


def tap_table():
    frac_part = jnp.arange(FRAC, dtype=jnp.float32)[:, None] / FRAC
    shift = jnp.arange(TAPS, dtype=jnp.float32)[None, :] - (TAPS // 2 - 1)
    offset = shift - frac_part
    values = jnp.sinc(offset) * (0.5 + 0.5 * jnp.cos(math.pi * offset / (TAPS // 2)))
    values = values / jnp.sum(values, axis=1, keepdims=True)
    return values.reshape(1, FRAC * TAPS)


def lane_take(row, index):
    return jnp.take_along_axis(row, index, axis=1, mode="promise_in_bounds")


def spread(row):
    return jnp.broadcast_to(row, (SUBLANES, LANES))


def cos_sin(steps):
    quarter = (steps + 512) >> 10
    x = (steps - (quarter << 10)).astype(jnp.float32) * (2.0 * math.pi / 4096.0)
    y = x * x
    s = x * (1.0 + y * (-1.0 / 6.0 + y * (1.0 / 120.0 + y * (-1.0 / 5040.0 + y * (1.0 / 362880.0)))))
    c = 1.0 + y * (-0.5 + y * (1.0 / 24.0 + y * (-1.0 / 720.0 + y * (1.0 / 40320.0))))
    odd = (quarter & 1) == 1
    cosine = jnp.where(odd, s, c)
    sine = jnp.where(odd, c, s)
    cosine = jnp.where(((quarter + 1) & 2) == 2, -cosine, cosine)
    sine = jnp.where((quarter & 2) == 2, -sine, sine)
    return cosine, sine


def arrange_kernel(shard_ref, bins_ref, offsets_ref, *refs):
    *index_refs, out_ref, tiles = refs
    near = lax.axis_index("near")
    lane = lax.broadcasted_iota(jnp.int32, (SUBLANES, LANES), 1)
    source = (lane & 15) * TAPS
    part = lane >> 4
    each = out_ref.shape[2]
    for c in range(2):
        rows = [shard_ref[c, :, t * LANES : (t + 1) * LANES] for t in range(TAPS)]
        for v in range(TAPS):
            got = lane_take(rows[0], source + v)
            for t in range(1, TAPS):
                got = jnp.where(part == t, lane_take(rows[t], source + v), got)
            tiles[c, :, v, :] = got
    quarters = SUBLANES // each
    length = index_refs[0].shape[2]
    for step, index_ref in enumerate(index_refs):
        for k, ref in enumerate((bins_ref, offsets_ref)):
            for p in range(each):
                pulse = pl.ds((near ^ step) * each + p, 1)
                for q in range(quarters):
                    row = p * quarters + q
                    index_ref[k, row : row + 1, :] = ref[pulse, q * length : (q + 1) * length]
    for c in range(2):
        for place in range(SIDE):
            for p in range(each):
                tile = tiles[c, place * each + p]
                for far in range(SIDE):
                    out_ref[SIDE * SIDE - 1 - (far * SIDE + place), c, p] = tile


def first_bins(index_ref):
    _, rows, length = index_ref.shape
    column = lax.broadcasted_iota(jnp.int32, (rows, LANES), 1)
    firsts = jnp.zeros((rows, LANES), jnp.int32)
    for block in range(length // BLOCK):
        bins = index_ref[0, :, block * BLOCK : (block + 1) * BLOCK].astype(jnp.float32)
        lowest = jnp.min(jnp.minimum(bins[:, :LANES], bins[:, LANES:]), axis=1, keepdims=True)
        firsts = jnp.where(column == block, lowest.astype(jnp.int32), firsts)
    return firsts


def prepare_kernel(scale, table_ref, index_ref, *refs):
    *before, first_ref, real_ref, imag_ref, lane_ref = refs[:-2] if len(refs) > 4 else refs
    _, rows, length = index_ref.shape
    firsts = first_bins(index_ref)
    if before:
        gathered_ref, sem = refs[-2:]
        for tile, firsts_ref in enumerate(before):
            mine = firsts_ref[:, :]
            shift = tile * (length // BLOCK)
            gathered = mine if tile == 0 else gathered + pltpu.roll(mine, shift, 1)
        gathered_ref[:, :] = gathered + pltpu.roll(firsts, len(before) * (length // BLOCK), 1)
        copy = pltpu.make_async_copy(gathered_ref, first_ref, sem)
        copy.start()
    else:
        first_ref[:, :] = firsts
    table = spread(table_ref[:, :])
    phase = lax.broadcasted_iota(jnp.int32, (SUBLANES, LANES), 0)
    for part in range(length // LANES):
        lanes = pl.ds(part * LANES, LANES)
        fine = index_ref[0, :, lanes] * FRAC + index_ref[1, :, lanes]
        cosine, sine = cos_sin((fine * 2861) & 4095)
        cosine, sine = cosine * scale, sine * scale
        for s in range(rows):
            fine_s = spread(fine[s : s + 1])
            bins_s = fine_s >> 4
            weight = lane_take(table, ((fine_s & 15) << 3) + ((phase - bins_s) & 7))
            real_ref[s, part] = weight * spread(cosine[s : s + 1])
            imag_ref[s, part] = weight * spread(sine[s : s + 1])
            lane_ref[s, part] = ((bins_s - phase + 7) >> 3) & (LANES - 1)
    if before:
        copy.wait()


def row_sums(values):
    row = lax.broadcasted_iota(jnp.int32, (SUBLANES, LANES), 0)
    low = (row & 4) == 0
    values = [jnp.where(low, a, b) + pltpu.roll(jnp.where(low, b, a), 4, 0) for a, b in zip(values[:4], values[4:])]
    for step in (2, 1):
        low = (row & step) == 0
        values = [
            jnp.where(low, a + pltpu.roll(a, SUBLANES - step, 0), b + pltpu.roll(b, step, 0))
            for a, b in zip(values[:step], values[step:])
        ]
    return values[0]


def project_kernel(own, first_ref, whole, *refs):
    real_refs, imag_refs, lane_refs, out_ref = refs[0:-1:3], refs[1:-1:3], refs[2:-1:3], refs[-1]
    tiles = len(real_refs)
    rows, parts = real_refs[0].shape[:2]
    owners, _, each = whole.shape[:3]
    quarters = rows // each
    halves = BLOCK // LANES
    near, core = lax.axis_index("near"), lax.axis_index("core")
    parity = core if own else 1 - core
    column = lax.broadcasted_iota(jnp.int32, (SUBLANES, LANES), 1)
    for tile in range(tiles):
        for quarter in range(quarters):
            sums = []
            for pair in range(parts // halves // 2):
                block = 2 * pair + parity
                total = [[jnp.zeros((SUBLANES, LANES), jnp.float32) for _ in range(halves)] for _ in range(2)]
                for p in range(each):
                    row = p * quarters + quarter
                    first = first_ref[row, tile * (parts // halves) + block]
                    owner = first >> 10
                    after = jnp.minimum(owner + 1, owners - 1)
                    here = column >= ((first >> 3) & (LANES - 1))
                    table = [jnp.where(here, whole[owners - 1 - owner, c, p], whole[owners - 1 - after, c, p]) for c in range(2)]
                    for half in range(halves):
                        part = block * halves + half
                        lane = lane_refs[tile][row, part]
                        got = [lane_take(table[c], lane) for c in range(2)]
                        real, imag = real_refs[tile][row, part], imag_refs[tile][row, part]
                        total[0][half] = total[0][half] + (got[0] * real - got[1] * imag)
                        total[1][half] = total[1][half] + (got[0] * imag + got[1] * real)
                sums = total[0] + total[1] + sums
            out_ref[tiles * quarters - 1 - ((STEPS[tile] ^ near) * quarters + quarter)] = row_sums(sums)


def swap(value, step):
    return lax.ppermute(value, "near", [(i, i ^ step) for i in range(SIDE)])


def backward(value, axes):
    return lax.all_to_all(value, axes, 0, 0, tiled=True, axis_index_groups=[list(range(value.shape[0]))[::-1]])


def local(profile, base_bin, tap_offset):
    pulses, pixels = base_bin.shape
    bins = profile.shape[2]
    each = pulses // SIDE
    quarters = SUBLANES // each
    length = pixels // quarters
    blocks, parts = length // BLOCK, length // LANES
    scale = 1.0 / math.sqrt(pulses * lax.axis_size(("x", "pair", "core")))
    vmem = pl.BlockSpec(memory_space=pltpu.VMEM)
    smem = pl.BlockSpec(memory_space=pltpu.SMEM)

    *index, shards = pl.pallas_call(
        arrange_kernel,
        out_shape=[jax.ShapeDtypeStruct((2, SUBLANES, length), jnp.int32)] * SIDE
        + [jax.ShapeDtypeStruct((SIDE * SIDE, 2, each, TAPS, bins // TAPS), jnp.float32)],
        in_specs=[vmem] * 3,
        out_specs=[vmem] * (SIDE + 1),
        scratch_shapes=[pltpu.VMEM((2, pulses, TAPS, bins // TAPS), jnp.float32)],
        compiler_params=pltpu.CompilerParams(vmem_limit_bytes=4 << 20),
        name="arrange",
    )(*(pltpu.with_memory_space_constraint(value, pltpu.HBM) for value in (profile, base_bin, tap_offset)))
    whole = backward(shards, ("far", "near"))
    index = [index[0]] + [swap(index[step], step) for step in STEPS[1:]]

    table = tap_table()
    prepared, firsts = [], []
    for tile in range(SIDE):
        last = tile == SIDE - 1
        first, *rest = pl.pallas_call(
            lambda *refs: prepare_kernel(scale, *refs),
            out_shape=[pltpu.SMEM((SUBLANES, LANES), jnp.int32) if last else jax.ShapeDtypeStruct((SUBLANES, LANES), jnp.int32)]
            + [jax.ShapeDtypeStruct((SUBLANES, parts, TAPS, LANES), kind) for kind in (jnp.float32, jnp.float32, jnp.int32)],
            in_specs=[vmem] * (2 + SIDE - 1 if last else 2),
            out_specs=[smem if last else vmem] + [vmem] * 3,
            scratch_shapes=[pltpu.VMEM((SUBLANES, LANES), jnp.int32), pltpu.SemaphoreType.DMA] if last else [],
            cost_estimate=pl.CostEstimate(flops=pulses * pixels * 75, bytes_accessed=pulses * pixels * 26, transcendentals=0),
            compiler_params=pltpu.CompilerParams(vmem_limit_bytes=16 << 20),
            name="prepare",
        )(table, index[tile], *(firsts if last else []))
        firsts.append(first)
        prepared += rest

    def project(own):
        return pl.pallas_call(
            lambda *refs: project_kernel(own, *refs),
            out_shape=jax.ShapeDtypeStruct((SIDE * quarters, SUBLANES, LANES), jnp.float32),
            in_specs=[smem] + [vmem] * (1 + 3 * SIDE),
            out_specs=vmem,
            cost_estimate=pl.CostEstimate(flops=1 << 24, bytes_accessed=2 << 20, transcendentals=0),
            compiler_params=pltpu.CompilerParams(vmem_limit_bytes=24 << 20),
            name="project",
        )(first, whole, *prepared)

    theirs = lax.ppermute(project(False), "core", [(0, 1), (1, 0)])
    partial_image = (project(True) + theirs).reshape(SIDE * pixels // BLOCK // 2, 2 * BLOCK // LANES, LANES)
    received = backward(partial_image, ("near", "x", "pair"))
    return jnp.sum(received, axis=0).reshape(2, BLOCK)


def solution(mesh):
    inner = Mesh(mesh.devices.reshape(SIZES), AXES)
    pulse, tile = ("x", "pair", "core"), ("far", "near")
    return jax.shard_map(
        local,
        mesh=inner,
        in_specs=(P(None, pulse, tile), P(pulse, tile), P(pulse, tile)),
        out_specs=P(None, tile + pulse),
        check_vma=False,
    )
```

```python
import math

import jax
import jax.numpy as jnp
from jax import lax
from jax.experimental import pallas as pl
from jax.experimental.pallas import tpu as pltpu
from jax.sharding import Mesh
from jax.sharding import PartitionSpec as P

TAPS = 8
FRAC = 16
BLOCK = 256
LANES = 128
SUBLANES = 8
SIDE = 4
STEPS = (0, 3, 2, 1)
START = 20
AXES = ("far", "near", "x", "pair", "core")
SIZES = (4, 4, 4, 2, 2)


def tap_table():
    frac_part = jnp.arange(FRAC, dtype=jnp.float32)[:, None] / FRAC
    shift = jnp.arange(TAPS, dtype=jnp.float32)[None, :] - (TAPS // 2 - 1)
    offset = shift - frac_part
    values = jnp.sinc(offset) * (0.5 + 0.5 * jnp.cos(math.pi * offset / (TAPS // 2)))
    values = values / jnp.sum(values, axis=1, keepdims=True)
    return values.reshape(1, FRAC * TAPS)


def lane_take(row, index):
    return jnp.take_along_axis(row, index, axis=1, mode="promise_in_bounds")


def spread(row):
    return jnp.broadcast_to(row, (SUBLANES, LANES))


def cos_sin(steps):
    quarter = (steps + 512) >> 10
    x = (steps - (quarter << 10)).astype(jnp.float32) * (2.0 * math.pi / 4096.0)
    y = x * x
    s = x * (1.0 + y * (-1.0 / 6.0 + y * (1.0 / 120.0 + y * (-1.0 / 5040.0 + y * (1.0 / 362880.0)))))
    c = 1.0 + y * (-0.5 + y * (1.0 / 24.0 + y * (-1.0 / 720.0 + y * (1.0 / 40320.0))))
    odd = (quarter & 1) == 1
    cosine = jnp.where(odd, s, c)
    sine = jnp.where(odd, c, s)
    cosine = jnp.where(((quarter + 1) & 2) == 2, -cosine, cosine)
    sine = jnp.where((quarter & 2) == 2, -sine, sine)
    return cosine, sine


def arrange_kernel(shard_ref, bins_ref, offsets_ref, *refs):
    *index_refs, out_ref, tiles = refs
    near = lax.axis_index("near")
    lane = lax.broadcasted_iota(jnp.int32, (SUBLANES, LANES), 1)
    source = (lane & 15) * TAPS
    part = lane >> 4
    each = out_ref.shape[2]
    for c in range(2):
        rows = [shard_ref[c, :, t * LANES : (t + 1) * LANES] for t in range(TAPS)]
        for v in range(TAPS):
            got = lane_take(rows[0], source + v)
            for t in range(1, TAPS):
                got = jnp.where(part == t, lane_take(rows[t], source + v), got)
            tiles[c, :, v, :] = got
    quarters = SUBLANES // each
    length = index_refs[0].shape[2]
    for step, index_ref in enumerate(index_refs):
        for k, ref in enumerate((bins_ref, offsets_ref)):
            for p in range(each):
                pulse = pl.ds((near ^ step) * each + p, 1)
                for q in range(quarters):
                    row = p * quarters + q
                    index_ref[k, row : row + 1, :] = ref[pulse, q * length : (q + 1) * length]
    for c in range(2):
        for place in range(SIDE):
            for p in range(each):
                tile = tiles[c, place * each + p]
                for far in range(SIDE):
                    out_ref[SIDE * SIDE - 1 - (far * SIDE + place), c, p] = tile


def first_bins(index_ref):
    _, rows, length = index_ref.shape
    column = lax.broadcasted_iota(jnp.int32, (rows, LANES), 1)
    firsts = jnp.zeros((rows, LANES), jnp.int32)
    for block in range(length // BLOCK):
        bins = index_ref[0, :, block * BLOCK : (block + 1) * BLOCK].astype(jnp.float32)
        lowest = jnp.min(jnp.minimum(bins[:, :LANES], bins[:, LANES:]), axis=1, keepdims=True)
        firsts = jnp.where(column == block, lowest.astype(jnp.int32), firsts)
    return firsts


def prepare_kernel(scale, table_ref, index_ref, *refs):
    *before, first_ref, real_ref, imag_ref, lane_ref = refs[:-2] if len(refs) > 4 else refs
    _, rows, length = index_ref.shape
    firsts = first_bins(index_ref)
    if before:
        gathered_ref, sem = refs[-2:]
        for tile, firsts_ref in enumerate(before):
            mine = firsts_ref[:, :]
            shift = tile * (length // BLOCK)
            gathered = mine if tile == 0 else gathered + pltpu.roll(mine, shift, 1)
        gathered_ref[:, :] = gathered + pltpu.roll(firsts, len(before) * (length // BLOCK), 1)
        copy = pltpu.make_async_copy(gathered_ref, first_ref, sem)
        copy.start()
    else:
        first_ref[:, :] = firsts
    table = spread(table_ref[:, :])
    phase = lax.broadcasted_iota(jnp.int32, (SUBLANES, LANES), 0)
    for part in range(length // LANES):
        lanes = pl.ds(part * LANES, LANES)
        fine = index_ref[0, :, lanes] * FRAC + index_ref[1, :, lanes]
        cosine, sine = cos_sin((fine * 2861) & 4095)
        cosine, sine = cosine * scale, sine * scale
        for s in range(rows):
            fine_s = spread(fine[s : s + 1])
            bins_s = fine_s >> 4
            weight = lane_take(table, ((fine_s & 15) << 3) + ((phase - bins_s) & 7))
            real_ref[s, part] = weight * spread(cosine[s : s + 1])
            imag_ref[s, part] = weight * spread(sine[s : s + 1])
            lane_ref[s, part] = ((bins_s - phase + 7) >> 3) & (LANES - 1)
    if before:
        copy.wait()


def row_sums(values):
    row = lax.broadcasted_iota(jnp.int32, (SUBLANES, LANES), 0)
    low = (row & 4) == 0
    values = [jnp.where(low, a, b) + pltpu.roll(jnp.where(low, b, a), 4, 0) for a, b in zip(values[:4], values[4:])]
    for step in (2, 1):
        low = (row & step) == 0
        values = [
            jnp.where(low, a + pltpu.roll(a, SUBLANES - step, 0), b + pltpu.roll(b, step, 0))
            for a, b in zip(values[:step], values[step:])
        ]
    return values[0]


def project_kernel(own, first_ref, whole, *refs):
    real_refs, imag_refs, lane_refs, out_ref = refs[0:-1:3], refs[1:-1:3], refs[2:-1:3], refs[-1]
    tiles = len(real_refs)
    rows, parts = real_refs[0].shape[:2]
    owners, _, each = whole.shape[:3]
    quarters = rows // each
    halves = BLOCK // LANES
    near, core = lax.axis_index("near"), lax.axis_index("core")
    parity = core if own else 1 - core
    column = lax.broadcasted_iota(jnp.int32, (SUBLANES, LANES), 1)
    for tile in range(tiles):
        for quarter in range(quarters):
            sums = []
            for pair in range(parts // halves // 2):
                block = 2 * pair + parity
                total = [[jnp.zeros((SUBLANES, LANES), jnp.float32) for _ in range(halves)] for _ in range(2)]
                for p in range(each):
                    row = p * quarters + quarter
                    first = first_ref[row, tile * (parts // halves) + block]
                    owner = first >> 10
                    after = jnp.minimum(owner + 1, owners - 1)
                    here = column >= ((first >> 3) & (LANES - 1))
                    table = [jnp.where(here, whole[owners - 1 - owner, c, p], whole[owners - 1 - after, c, p]) for c in range(2)]
                    for half in range(halves):
                        part = block * halves + half
                        lane = lane_refs[tile][row, part]
                        got = [lane_take(table[c], lane) for c in range(2)]
                        real, imag = real_refs[tile][row, part], imag_refs[tile][row, part]
                        total[0][half] = total[0][half] + (got[0] * real - got[1] * imag)
                        total[1][half] = total[1][half] + (got[0] * imag + got[1] * real)
                sums = sums + total[0] + total[1]
            out_ref[((STEPS[tile] ^ near) * quarters + quarter - START // 2) & (tiles * quarters - 1)] = row_sums(sums)


def swap(value, step):
    return lax.ppermute(value, "near", [(i, i ^ step) for i in range(SIDE)])


def backward(value, axes):
    return lax.all_to_all(value, axes, 0, 0, tiled=True, axis_index_groups=[list(range(value.shape[0]))[::-1]])


def local(profile, base_bin, tap_offset):
    pulses, pixels = base_bin.shape
    bins = profile.shape[2]
    each = pulses // SIDE
    quarters = SUBLANES // each
    length = pixels // quarters
    blocks, parts = length // BLOCK, length // LANES
    scale = 1.0 / math.sqrt(pulses * lax.axis_size(("x", "pair", "core")))
    vmem = pl.BlockSpec(memory_space=pltpu.VMEM)
    smem = pl.BlockSpec(memory_space=pltpu.SMEM)

    *index, shards = pl.pallas_call(
        arrange_kernel,
        out_shape=[jax.ShapeDtypeStruct((2, SUBLANES, length), jnp.int32)] * SIDE
        + [jax.ShapeDtypeStruct((SIDE * SIDE, 2, each, TAPS, bins // TAPS), jnp.float32)],
        in_specs=[vmem] * 3,
        out_specs=[vmem] * (SIDE + 1),
        scratch_shapes=[pltpu.VMEM((2, pulses, TAPS, bins // TAPS), jnp.float32)],
        compiler_params=pltpu.CompilerParams(vmem_limit_bytes=4 << 20),
        name="arrange",
    )(*(pltpu.with_memory_space_constraint(value, pltpu.HBM) for value in (profile, base_bin, tap_offset)))
    whole = backward(shards, ("far", "near"))
    index = [index[0]] + [swap(index[step], step) for step in STEPS[1:]]

    table = tap_table()
    prepared, firsts = [], []
    for tile in range(SIDE):
        last = tile == SIDE - 1
        first, *rest = pl.pallas_call(
            lambda *refs: prepare_kernel(scale, *refs),
            out_shape=[pltpu.SMEM((SUBLANES, LANES), jnp.int32) if last else jax.ShapeDtypeStruct((SUBLANES, LANES), jnp.int32)]
            + [jax.ShapeDtypeStruct((SUBLANES, parts, TAPS, LANES), kind) for kind in (jnp.float32, jnp.float32, jnp.int32)],
            in_specs=[vmem] * (2 + SIDE - 1 if last else 2),
            out_specs=[smem if last else vmem] + [vmem] * 3,
            scratch_shapes=[pltpu.VMEM((SUBLANES, LANES), jnp.int32), pltpu.SemaphoreType.DMA] if last else [],
            cost_estimate=pl.CostEstimate(flops=pulses * pixels * 75, bytes_accessed=pulses * pixels * 26, transcendentals=0),
            compiler_params=pltpu.CompilerParams(vmem_limit_bytes=16 << 20),
            name="prepare",
        )(table, index[tile], *(firsts if last else []))
        firsts.append(first)
        prepared += rest

    def project(own):
        return pl.pallas_call(
            lambda *refs: project_kernel(own, *refs),
            out_shape=jax.ShapeDtypeStruct((SIDE * quarters, SUBLANES, LANES), jnp.float32),
            in_specs=[smem] + [vmem] * (1 + 3 * SIDE),
            out_specs=vmem,
            cost_estimate=pl.CostEstimate(flops=1 << 24, bytes_accessed=2 << 20, transcendentals=0),
            compiler_params=pltpu.CompilerParams(vmem_limit_bytes=24 << 20),
            name="project",
        )(first, whole, *prepared)

    theirs = lax.ppermute(project(False), "core", [(0, 1), (1, 0)])
    partial_image = (project(True) + theirs).reshape(SIDE * pixels // BLOCK // 2, 2 * BLOCK // LANES, LANES)
    count = partial_image.shape[0]
    order = [(START + i) % count for i in range(count)]
    received = lax.all_to_all(partial_image, ("near", "x", "pair"), 0, 0, tiled=True, axis_index_groups=[order])
    return jnp.sum(received, axis=0).reshape(2, BLOCK)


def solution(mesh):
    inner = Mesh(mesh.devices.reshape(SIZES), AXES)
    pulse, tile = ("x", "pair", "core"), ("far", "near")
    return jax.shard_map(
        local,
        mesh=inner,
        in_specs=(P(None, pulse, tile), P(pulse, tile), P(pulse, tile)),
        out_specs=P(None, tile + pulse),
        check_vma=False,
    )
```
